256 devices in a mesh: dp: 32 (over y, x, core), tensor: 8 (over z).
Axes of the slice: x: 4, y: 4, z: 8, core: 2. Of those that a mesh axis runs over, the one named last changes fastest.
Arguments:
- tokens: bfloat16 [16384, 5120], P(('dp', 'tensor')), may hold values from -6 to 6
- token_grads: bfloat16 [16384, 3072], P('dp', 'tensor'), may hold values from -0.625 to 0.625
- weight: bfloat16 [5120, 3072], P(None, 'tensor'), may hold values from -6 to 6
- feedback: bfloat16 [32, 5120, 3072], P('dp', None, 'tensor'), may hold values from -6 to 6
- q_start: float32 [3072, 32], P('tensor'), may hold values from -6 to 6
Outputs:
- input_grads: bfloat16 [16384, 5120], P(('dp', 'tensor'))
- new_feedback: bfloat16 [32, 5120, 3072], P('dp', None, 'tensor')
- q_next: float32 [3072, 32], P('tensor')
The draws below stay inside these ranges and needn't reach their ends.
All inputs are finite; a program needn't handle non-finite values.
Results may differ from the reference program's by a relative error of at most 0.019.
Values may be sent and summed in bfloat16 or wider, within the bound.
A program may use at most 128 MiB of HBM per device.

```python
import jax
import jax.numpy as jnp
from jax import lax

D = 5120
R = 32
TOK = 512
HD = 3072
TOKENS = 16384
N_DP = 32
N_TENSOR = 8


def block_levels(own_key, shape, split, smallest, top_value):
    def one(position, shards_of):
        steps = jax.random.uniform(jax.random.fold_in(jax.random.fold_in(own_key, 6), position), (shards_of,), jnp.float32, smallest / len(split), top_value / len(split))
        return jnp.repeat(jnp.exp(steps), shape[position] // shards_of).reshape((-1,) + (1,) * (len(shape) - position - 1))

    gain = one(*split[0])
    for cut in split[1:]:
        gain = gain * one(*cut)
    return gain


def bell_draw(key, shape, deviation, reach, shards=(), kind=jnp.bfloat16):
    gain = block_levels(key, shape, shards, -0.22, 0.18) if shards else 1.0
    result = jax.random.normal(key, shape, jnp.float32) * deviation * gain
    return jnp.minimum(jnp.maximum(result, -reach), reach).astype(kind)


def setup_inputs(seed: int = 0) -> dict:
    streams_of = jax.random.split(jax.random.key(seed), 6)
    return {
        "tokens": bell_draw(streams_of[0], (TOKENS, D), 1.0, 6.0, ((0, 256),)),
        "token_grads": bell_draw(streams_of[1], (TOKENS, HD), (TOK ** -0.5), 0.625, ((0, 32), (1, 8))),
        "weight": bell_draw(streams_of[2], (D, HD), (TOK ** 0.5 * HD ** -0.5), 6.0, ((1, 8),)),
        "feedback": bell_draw(streams_of[3], (N_DP, D, HD), 1.0, 6.0, ((0, 32), (2, 8))),
        "q_start": bell_draw(streams_of[4], (HD, R), 1.0, 6.0, ((0, 8),), jnp.float32),
    }


def orthonormal(p_sum):
    gram_matrix = jnp.dot(p_sum.T, p_sum, precision=lax.Precision.HIGHEST)
    factor_low = jnp.linalg.cholesky(gram_matrix)
    return jax.scipy.linalg.solve_triangular(factor_low, p_sum.T, lower=True).T

def reference(tokens, token_grads, weight, feedback, q_start):
    width_share = HD // N_TENSOR
    grad_blocks = token_grads.reshape(TOKENS, N_TENSOR, width_share).transpose(1, 0, 2)
    weight_blocks = weight.reshape(D, N_TENSOR, width_share).transpose(1, 0, 2)

    def add_partial(carry, pair):
        partial_value = lax.dot_general(pair[0].astype(jnp.float32), pair[1].astype(jnp.float32), (((1,), (1,)), ((), ())), preferred_element_type=jnp.float32)
        rounded = lax.optimization_barrier(partial_value.astype(jnp.bfloat16))
        return (carry + rounded.astype(jnp.float32), None)
    grad_total, _ = lax.scan(add_partial, jnp.zeros((TOKENS, D), jnp.float32), (grad_blocks, weight_blocks))
    input_grads = grad_total.astype(jnp.bfloat16)
    tokens_split = tokens.reshape(N_DP, TOK, D)
    grads_split = token_grads.reshape(N_DP, TOK, HD)
    indices = jnp.arange(N_DP, dtype=jnp.int32)

    def merged_of(index):
        gradient = lax.dot_general(tokens_split[index].astype(jnp.float32), grads_split[index].astype(jnp.float32), (((0,), (0,)), ((), ())), preferred_element_type=jnp.float32)
        return gradient + feedback[index].astype(jnp.float32)

    def add_left(carry, index):
        return (carry + jnp.dot(merged_of(index), q_start, precision=lax.Precision.HIGHEST), None)
    p_sum, _ = lax.scan(add_left, jnp.zeros((D, R), jnp.float32), indices)
    p_hat = orthonormal(p_sum)

    def add_right(carry, index):
        return (carry + jnp.dot(merged_of(index).T, p_hat, precision=lax.Precision.HIGHEST), None)
    q_total, _ = lax.scan(add_right, jnp.zeros((HD, R), jnp.float32), indices)
    q_next = q_total / N_DP
    decompressed = jnp.dot(p_hat, q_next.T, precision=lax.Precision.HIGHEST)
    new_feedback = lax.map(lambda index: (merged_of(index) - decompressed).astype(jnp.bfloat16), indices)
    return (input_grads, new_feedback, q_next)
```

```python
import functools

import jax
import jax.numpy as jnp
from jax import lax
from jax.experimental import pallas as pl
from jax.experimental.pallas import tpu as pltpu
from jax.sharding import PartitionSpec as P

MESH = pl.DeviceIdType.MESH
F32 = jnp.float32
BF16 = jnp.bfloat16
NY, NX, NZ = 4, 4, 8
NP = NY * NX
R = 32
NN = (((1,), (0,)), ((), ()))
NT = (((1,), (1,)), ((), ()))
TN = (((0,), (0,)), ((), ()))


def mm(a, b, dims):
    return lax.dot_general(a, b, dims, preferred_element_type=F32)


def split3(v):
    hi = v.astype(BF16)
    rest = v - hi.astype(F32)
    mid = rest.astype(BF16)
    low = (rest - mid.astype(F32)).astype(BF16)
    return hi, mid, low


def stack3(v):
    return jnp.concatenate(split3(v), axis=0)


def fold3(v):
    return v[0:R] + v[R : 2 * R] + v[2 * R : 3 * R]


def inverse_factor(gram):
    rows = lax.broadcasted_iota(jnp.int32, (R, 1), 0)
    eye = (
        lax.broadcasted_iota(jnp.int32, (R, R), 0)
        == lax.broadcasted_iota(jnp.int32, (R, R), 1)
    ).astype(F32)
    a = jnp.concatenate([gram, eye], axis=1)
    for j in range(R):
        row = a[j : j + 1, :]
        pivot = a[j : j + 1, j : j + 1]
        factor = jnp.where(rows > j, a[:, j : j + 1] / pivot, 0.0)
        a = a - factor * row
    diag = jnp.sum(a[:, :R] * eye, axis=1, keepdims=True)
    return a[:, R:] / jnp.sqrt(diag)


def main_kernel(
    x_ref, g_ref, q_ref, w_hbm, f_hbm,
    ig_ref, ps_out, qs_out, qn_out,
    f_ref, hb, hr, pb, pcr, ph, ppr, zb, pzr, pfin, ps, yb, yr, qb, qcr, qp, qfin, ga, wa, ob,
    lsem, hs, hrs, cs, crs, rss, rsr, zs, zr, ags, agr, ys, yrs, qps, qpr_s,
    gas, gar, gxs, gxr, gss, gsr, wzs, wzr, wys, wyr, oxs, oxr,
):
    dp = lax.axis_index("dp")
    z = lax.axis_index("tensor")
    plane = dp // 2
    core = lax.rem(dp, 2)
    y, x = plane // NX, lax.rem(plane, NX)
    sign = 1 - 2 * core
    seat = 2 * x + core

    def at(yy, xx, cc, zz):
        return ((yy * NX + xx) * 2 + cc, zz)

    def z_of(k):
        return lax.rem(z + k + 2 * NZ, NZ)

    def x_of(k):
        return lax.rem(x + k + 2 * NX, NX)

    def y_of(k):
        return lax.rem(y + k + 2 * NY, NY)

    def p_of(k):
        return lax.rem(plane + k, NP)

    def rcopy(src, dst, s_sem, r_sem, device):
        return pltpu.make_async_remote_copy(
            src_ref=src, dst_ref=dst, send_sem=s_sem, recv_sem=r_sem,
            device_id=device, device_id_type=MESH,
        )

    sent = []

    def go(copy):
        copy.start()
        sent.append(copy)
        return copy

    sibling = (2 * plane + 1 - core, z)

    f_copies = []
    for i in range(2):
        part = pl.ds(2560 * i, 2560)
        f_copies.append(pltpu.make_async_copy(f_hbm.at[part], f_ref.at[part], lsem.at[i]))
        f_copies[-1].start()

    barrier = pltpu.get_barrier_semaphore()
    peers = [(dp, z_of(k)) for k in range(1, NZ)]
    peers += [(2 * p_of(k) + core, z) for k in range(1, NP)]
    peers += [at(y, x_of(k), 1 - core, z) for k in range(NX)]
    for peer in peers:
        pl.semaphore_signal(barrier, 1, device_id=peer, device_id_type=MESH)

    qs = stack3(q_ref[...].T)
    hfull = fold3(mm(qs, g_ref[...], NT))
    for t in range(4):
        hb[t] = hfull[:, 128 * t : 128 * t + 128]
    pl.semaphore_wait(barrier, len(peers))

    h_copies = []
    for k in range(1, NZ):
        zd = z_of(k)
        h_copies.append(go(rcopy(hb.at[zd // 2], hr.at[k], hs.at[k], hrs.at[k], (dp, zd))))

    def g_rows(s):
        return pl.ds(pl.multiple_of(64 * s, 64), 64)

    def lanes(zz):
        return pl.ds(pl.multiple_of(384 * zz, 128), 384)

    ga_copies = []
    for k in range(1, NZ):
        zd = z_of(k)
        ga_copies.append(
            go(rcopy(g_ref.at[g_rows(zd), :], ga.at[g_rows(seat), lanes(z)], gas.at[k], gar.at[k], (dp, zd)))
        )
    ga[g_rows(seat), lanes(z)] = g_ref[g_rows(z), :]

    def w_rows(yy):
        return pl.ds(pl.multiple_of(160 * yy, 32), 160)

    own_w = w_hbm.at[pl.ds(pl.multiple_of(640 * seat + 160 * y, 32), 160), :]
    own_slot = wa.at[w_rows(y), lanes(z)]
    w_local = pltpu.make_async_copy(own_w, own_slot, lsem.at[2])
    w_local.start()
    ring = [None] * 8

    def w_ring(step, toward, index):
        zz = z_of(-toward * step)
        slot = wa.at[w_rows(y), lanes(zz)]
        src = own_w if step == 0 else slot
        ring[index] = go(rcopy(src, slot, wzs.at[index], wzr.at[index], (dp, z_of(toward))))

    ydev = [at(y_of(sign), x, core, z), at(y_of(-sign), x, core, z)]
    ysent = {}

    def w_share(m, zz):
        slot = wa.at[w_rows(y), lanes(zz)]
        src = own_w if m == 0 else slot
        for i in range(2):
            ysent[m, i] = go(rcopy(src, slot, wys.at[m, i], wyr.at[m, i], ydev[i]))

    def w_relay(m, zz):
        ysent[m, 0].wait_recv()
        slot = wa.at[w_rows(y_of(-sign)), lanes(zz)]
        ysent[m, 2] = go(rcopy(slot, slot, wys.at[m, 2], wyr.at[m, 2], ydev[0]))

    z_from = [z] + [z_of(d * k * sign) for k in range(1, 4) for d in (-1, 1)] + [z_of(4)]

    def w_arrive(m):
        ring[m].wait_recv()
        k = (m + 1) // 2
        if m % 2 == 1 and k < 4:
            w_ring(k, sign, m + 2)
        if m % 2 == 0 and k < 3:
            w_ring(k, -sign, m + 2)
        w_share(m, z_from[m])

    w_ring(0, sign, 1)
    w_ring(0, -sign, 2)
    w_share(0, z)

    for c in f_copies:
        c.wait()

    def f_rows(cb):
        return pl.ds(pl.multiple_of(640 * cb, 640), 640)

    def x_lanes(cb):
        return pl.ds(pl.multiple_of(640 * cb, 128), 640)

    @pl.loop(0, 8)
    def _(cb):
        v = fold3(mm(qs, f_ref[f_rows(cb), :], NT))
        for a in range(4):
            pb[a, cb] = v[8 * a : 8 * a + 8]

    for c in h_copies:
        c.wait_recv()
    hsum = hb[z // 2]
    for k in range(1, NZ):
        hsum = hsum + hr[k]
    hsum = jnp.where(lax.rem(z, 2) == 1, pltpu.roll(hsum, 64, 1), hsum)
    hparts = stack3(hsum[:, :64])

    @pl.loop(0, 8)
    def _(cb):
        v = fold3(mm(hparts, x_ref[:, x_lanes(cb)], NN))
        for a in range(4):
            pb[a, cb] = pb[a, cb] + v[8 * a : 8 * a + 8]

    c_copy = go(rcopy(pb.at[pl.ds(2 * (1 - core), 2)], pcr, cs.at[0], crs.at[0], sibling))
    for c in ga_copies:
        c.wait_recv()
    block = ga.at[g_rows(seat), :]
    xdev = [at(y, x_of(sign), core, z), at(y, x_of(-sign), core, z)]
    gx = [go(rcopy(block, block, gxs.at[i], gxr.at[i], xdev[i])) for i in range(2)]
    gsib = [go(rcopy(block, block, gss.at[0], gsr.at[0], sibling))]
    c_copy.wait_recv()

    @pl.loop(0, 8)
    def _(cb):
        for hh in range(2):
            ph[8 * hh + cb] = pb[2 * core + hh, cb] + pcr[hh, cb]

    rs_copies = []
    for k in range(1, NP):
        pd = p_of(k)
        rs_copies.append(go(rcopy(ph.at[pd], ppr.at[k], rss.at[k], rsr.at[k], (2 * pd + core, z))))
    w_local.wait()
    w_arrive(1)
    w_arrive(2)
    for c in rs_copies:
        c.wait_recv()
    total = ph[plane]
    for k in range(1, NP):
        total = total + ppr[k]
    zb[...] = total
    z_copies = []
    for k in range(1, NZ):
        z_copies.append(go(rcopy(zb, pzr.at[k], zs.at[k], zr.at[k], (dp, z_of(k)))))
    w_arrive(3)
    w_arrive(4)
    for c in z_copies:
        c.wait_recv()
    for k in range(1, NZ):
        total = total + pzr[k]
    own_piece = pfin.at[core, plane]
    own_piece[...] = total
    ag_copies = []
    for k in range(1, NP):
        ag_copies.append(
            go(rcopy(own_piece, own_piece, ags.at[k], agr.at[k], (2 * p_of(k) + core, z)))
        )

    def g_block(xx):
        return ga.at[g_rows(2 * xx + core), :]

    def g_pass(i):
        gx[i].wait_recv()
        blk = g_block(x_of(-sign if i == 0 else (sign if i == 1 else 2)))
        if i == 0:
            gx.append(go(rcopy(blk, blk, gxs.at[2], gxr.at[2], xdev[0])))
        gsib.append(go(rcopy(blk, blk, gss.at[i + 1], gsr.at[i + 1], sibling)))

    g_pass(0)
    g_pass(1)
    for c in ag_copies:
        c.wait_recv()
    half = pfin.at[core]
    cg_copy = go(rcopy(half, half, cs.at[1], crs.at[1], sibling))
    w_arrive(5)
    w_arrive(6)
    cg_copy.wait_recv()

    def p_block(cb):
        return jnp.concatenate([pfin[a // 2, 8 * (a % 2) + cb] for a in range(4)], axis=0)

    def accumulate(cb, carry):
        gram, yt = carry
        parts = stack3(p_block(cb))
        ps[cb] = parts
        gram = gram + mm(parts, parts, NT)
        yt = yt + mm(parts, x_ref[:, x_lanes(cb)], NT)
        return gram, yt

    gram, yt = lax.fori_loop(
        0, 8, accumulate, (jnp.zeros((96, 96), F32), jnp.zeros((96, 64), F32))
    )
    yt = fold3(yt)
    yb[...] = jnp.concatenate([yt, jnp.zeros((R, 64), F32)], axis=1)
    y_copies = []
    for k in range(1, NZ):
        y_copies.append(go(rcopy(yb, yr.at[k], ys.at[k], yrs.at[k], (dp, z_of(k)))))

    qt = lax.fori_loop(
        0, 8, lambda cb, t: t + mm(ps[cb], f_ref[f_rows(cb), :], NN), jnp.zeros((96, 384), F32)
    )
    gram = fold3(gram)
    gram = gram[:, 0:R] + gram[:, R : 2 * R] + gram[:, 2 * R : 3 * R]
    linv = inverse_factor(gram)
    w_arrive(7)
    g_pass(2)

    qt = qt + mm(stack3(yt), g_ref[g_rows(z), :], NN)
    for k in range(1, NZ):
        y_copies[k - 1].wait_recv()
        qt = qt + mm(stack3(yr[k][:, :64]), g_ref[g_rows(z_of(-k)), :], NN)
    qt = fold3(qt)
    for cc in range(2):
        qb[cc] = qt[16 * cc : 16 * cc + 16]
    qc_copy = go(rcopy(qb.at[1 - core], qcr, cs.at[2], crs.at[2], sibling))
    l3 = split3(linv)
    lparts = jnp.concatenate([jnp.concatenate([part] * 3, axis=1) for part in l3], axis=0)
    qc_copy.wait_recv()
    own_q = qp.at[plane]
    own_q[...] = qb[core] + qcr[...]
    q_copies = []
    for k in range(1, NP):
        q_copies.append(go(rcopy(own_q, own_q, qps.at[k], qpr_s.at[k], (2 * p_of(k) + core, z))))

    @pl.loop(0, 8)
    def _(cb):
        hi, mid, low = split3(fold3(mm(lparts, ps[cb], NN)))
        ps_out[cb] = jnp.concatenate([hi, hi, hi, mid, mid, low], axis=0)

    for m in range(4):
        w_relay(m, z_from[m])
    for c in q_copies:
        c.wait_recv()
    qsum = qp[0]
    for p in range(1, NP):
        qsum = qsum + qp[p]
    own_half = qfin.at[core]
    own_half[...] = qsum
    qg_copy = go(rcopy(own_half, own_half, cs.at[3], crs.at[3], sibling))
    for m in range(4, 8):
        w_relay(m, z_from[m])
    qg_copy.wait_recv()
    qall = stack3(jnp.concatenate([qfin[0], qfin[1]], axis=0))
    qn = fold3(mm(lparts, qall, NN)) * (1.0 / 32.0)
    qn_out[...] = qn.T
    hi, mid, low = split3(-qn)
    qs_out[...] = jnp.concatenate([hi, mid, low, hi, mid, hi], axis=0)

    for c in gsib:
        c.wait_recv()
    for m in range(8):
        ysent[m, 1].wait_recv()
        ysent[m, 2].wait_recv()

    def ig_rows(i):
        return pl.ds(pl.multiple_of(128 * i, 128), 128)

    @pl.loop(0, 4)
    def _(i):
        ob[ig_rows(i), :] = mm(ga[ig_rows(i), :], wa[...], NT).astype(BF16)

    own_cols = pl.ds(pl.multiple_of(640 * seat, 128), 640)
    out = []
    for dx in range(NX):
        for other in range(2):
            if dx == 0 and other == 0:
                continue
            i = 2 * dx + other
            xd = x_of(dx)
            cd = core if other == 0 else 1 - core
            out.append(
                go(rcopy(ob.at[g_rows(2 * xd + cd), :], ig_ref.at[:, own_cols], oxs.at[i], oxr.at[i], at(y, xd, cd, z)))
            )
    ig_ref[:, own_cols] = ob[g_rows(seat), :]
    for c in out:
        c.wait_recv()
    for c in sent:
        c.wait_send()


def final_kernel(x_ref, p_ref, g_ref, q_ref, f_ref, o_ref):
    value = mm(x_ref[...], g_ref[...], TN) + mm(p_ref[0], q_ref[...], TN)
    o_ref[...] = (value + f_ref[...].astype(F32)).astype(BF16)


def local(tokens, token_grads, weight, feedback, q_start):
    vmem = pl.BlockSpec(memory_space=pltpu.VMEM)
    hbm = pl.BlockSpec(memory_space=pl.ANY)
    dma = pltpu.SemaphoreType.DMA
    carried = feedback[0]
    every = lax.all_gather(tokens, "tensor", axis=0, tiled=True)
    input_grads, p_parts, q_parts, q_next = pl.pallas_call(
        main_kernel,
        name="factors_and_input_grads",
        out_shape=(
            jax.ShapeDtypeStruct((64, 5120), BF16),
            jax.ShapeDtypeStruct((8, 192, 640), BF16),
            jax.ShapeDtypeStruct((192, 384), BF16),
            jax.ShapeDtypeStruct((384, R), F32),
        ),
        in_specs=[vmem, vmem, vmem, hbm, hbm],
        out_specs=(vmem, vmem, vmem, vmem),
        scratch_shapes=[
            pltpu.VMEM((5120, 384), BF16),
            pltpu.VMEM((4, R, 128), F32),
            pltpu.VMEM((NZ, R, 128), F32),
            pltpu.VMEM((4, 8, 8, 640), F32),
            pltpu.VMEM((2, 8, 8, 640), F32),
            pltpu.VMEM((NP, 8, 640), F32),
            pltpu.VMEM((NP, 8, 640), F32),
            pltpu.VMEM((8, 640), F32),
            pltpu.VMEM((NZ, 8, 640), F32),
            pltpu.VMEM((2, NP, 8, 640), F32),
            pltpu.VMEM((8, 96, 640), BF16),
            pltpu.VMEM((R, 128), F32),
            pltpu.VMEM((NZ, R, 128), F32),
            pltpu.VMEM((2, 16, 384), F32),
            pltpu.VMEM((16, 384), F32),
            pltpu.VMEM((NP, 16, 384), F32),
            pltpu.VMEM((2, 16, 384), F32),
            pltpu.VMEM((512, 3072), BF16),
            pltpu.VMEM((640, 3072), BF16),
            pltpu.VMEM((512, 640), BF16),
            dma((3,)),
            dma((NZ,)), dma((NZ,)),
            dma((4,)), dma((4,)),
            dma((NP,)), dma((NP,)),
            dma((NZ,)), dma((NZ,)),
            dma((NP,)), dma((NP,)),
            dma((NZ,)), dma((NZ,)),
            dma((NP,)), dma((NP,)),
            dma((NZ,)), dma((NZ,)),
            dma((3,)), dma((3,)),
            dma((4,)), dma((4,)),
            dma((8,)), dma((8,)),
            dma((8, 3)), dma((8, 3)),
            dma((8,)), dma((8,)),
        ],
        compiler_params=pltpu.CompilerParams(
            collective_id=0, has_side_effects=True, vmem_limit_bytes=48 * 2**20
        ),
        cost_estimate=pl.CostEstimate(flops=3 * 10**9, bytes_accessed=200 * 10**6, transcendentals=0),
    )(tokens, token_grads, q_start, weight, carried)
    new_feedback = pl.pallas_call(
        final_kernel,
        name="new_feedback",
        grid=(8,),
        out_shape=jax.ShapeDtypeStruct((5120, 384), BF16),
        in_specs=[
            pl.BlockSpec((512, 640), lambda i: (0, i)),
            pl.BlockSpec((1, 192, 640), lambda i: (i, 0, 0)),
            pl.BlockSpec((512, 384), lambda i: (0, 0)),
            pl.BlockSpec((192, 384), lambda i: (0, 0)),
            pl.BlockSpec((640, 384), lambda i: (i, 0)),
        ],
        out_specs=pl.BlockSpec((640, 384), lambda i: (i, 0)),
        compiler_params=pltpu.CompilerParams(vmem_limit_bytes=32 * 2**20),
        cost_estimate=pl.CostEstimate(
            flops=2 * 704 * 5120 * 384, bytes_accessed=15 * 10**6, transcendentals=0
        ),
    )(every, p_parts, token_grads, q_parts, carried)
    return input_grads, new_feedback[None], q_next


def solution(mesh):
    return jax.shard_map(
        local,
        mesh=mesh,
        in_specs=(
            P(("dp", "tensor"), None),
            P("dp", "tensor"),
            P(None, "tensor"),
            P("dp", None, "tensor"),
            P("tensor", None),
        ),
        out_specs=(P(("dp", "tensor"), None), P("dp", None, "tensor"), P("tensor", None)),
        check_vma=False,
    )
```

```python
import jax
import jax.numpy as jnp
from jax import lax
from jax.experimental import pallas as pl
from jax.experimental.pallas import tpu as pltpu
from jax.sharding import PartitionSpec as P

MESH = pl.DeviceIdType.MESH
F32 = jnp.float32
BF16 = jnp.bfloat16
NY, NX, NZ = 4, 4, 8
NP = NY * NX
R = 32
NN = (((1,), (0,)), ((), ()))
NT = (((1,), (1,)), ((), ()))
TN = (((0,), (0,)), ((), ()))


def mm(a, b, dims):
    return lax.dot_general(a, b, dims, preferred_element_type=F32)


def split3(v):
    hi = v.astype(BF16)
    rest = v - hi.astype(F32)
    mid = rest.astype(BF16)
    low = (rest - mid.astype(F32)).astype(BF16)
    return hi, mid, low


def stack3(v):
    return jnp.concatenate(split3(v), axis=0)


def fold3(v):
    return v[0:R] + v[R : 2 * R] + v[2 * R : 3 * R]


def inverse_factor(gram):
    rows = lax.broadcasted_iota(jnp.int32, (R, 1), 0)
    eye = (
        lax.broadcasted_iota(jnp.int32, (R, R), 0)
        == lax.broadcasted_iota(jnp.int32, (R, R), 1)
    ).astype(F32)
    a = jnp.concatenate([gram, eye], axis=1)
    for j in range(R):
        row = a[j : j + 1, :]
        pivot = a[j : j + 1, j : j + 1]
        factor = jnp.where(rows > j, a[:, j : j + 1] / pivot, 0.0)
        a = a - factor * row
    diag = jnp.sum(a[:, :R] * eye, axis=1, keepdims=True)
    return a[:, R:] / jnp.sqrt(diag)


def main_kernel(
    x_hbm, g_hbm, q_hbm, w_hbm, f_hbm,
    ig_ref, nf_ref, qn_ref,
    g_ref, q_ref, f_ref, xa, acc, pst, qst, hb, hr, pb, pcr, ph, ppr, zb, pzr, zf, pfin, ps, yb, yr,
    qb, qcr, qp, qfin, ga, wa, cols, ob,
    lsem, hs, hrs, cs, crs, rss, rsr, zs, zr, zgs, zgr, ags, agr, ys, yrs, qps, qpr_s,
    gas, gar, gxs, gxr, gss, gsr, wzs, wzr, wys, wyr, oxs, oxr, tls, tlr, tss, tsr,
):
    dp = lax.axis_index("dp")
    z = lax.axis_index("tensor")
    plane = dp // 2
    core = lax.rem(dp, 2)
    y, x = plane // NX, lax.rem(plane, NX)
    sign = 1 - 2 * core
    seat = 2 * x + core

    def at(yy, xx, cc, zz):
        return ((yy * NX + xx) * 2 + cc, zz)

    def z_of(k):
        return lax.rem(z + k + 2 * NZ, NZ)

    def x_of(k):
        return lax.rem(x + k + 2 * NX, NX)

    def y_of(k):
        return lax.rem(y + k + 2 * NY, NY)

    def p_of(k):
        return lax.rem(plane + k, NP)

    sent, pending = [], {}

    def go(src, dst, s_sem, r_sem, device):
        copy = pltpu.make_async_remote_copy(
            src_ref=src, dst_ref=dst, send_sem=s_sem, recv_sem=r_sem,
            device_id=device, device_id_type=MESH,
        )
        copy.start()
        sent.append(copy)
        pending[id(copy)] = copy
        return copy

    def got(copy):
        copy.wait_recv()
        del pending[id(copy)]

    sibling = (2 * plane + 1 - core, z)

    def g_rows(s):
        return pl.ds(pl.multiple_of(64 * s, 64), 64)

    def lanes(zz):
        return pl.ds(pl.multiple_of(384 * zz, 128), 384)

    def f_rows(cb):
        return pl.ds(pl.multiple_of(640 * cb, 640), 640)

    def x_lanes(cb):
        return pl.ds(pl.multiple_of(640 * cb, 128), 640)

    z_from = [z] + [z_of(d * k * sign) for k in range(1, 4) for d in (-1, 1)] + [z_of(4)]
    xdev = [at(y, x_of(sign), core, z), at(y, x_of(-sign), core, z)]
    ydev = [at(y_of(sign), x, core, z), at(y_of(-sign), x, core, z)]
    zdev = [(dp, z_of(sign)), (dp, z_of(-sign))]

    tl, ts = {}, {}

    def tick(t):
        k, part = t // 4, pl.ds(1280 * (t % 4), 1280)
        if k > 0:
            got(tl[t - 4])
        out = xa.at[z_of(-sign * k), :, part]
        tl[t] = go(out, out, tls.at[t], tlr.at[t], zdev[0])
        if k > 0 and t - 4 in ts:
            got(ts[t - 4])
        if k < 3:
            out = xa.at[z_of(sign * k), :, part]
            ts[t] = go(out, out, tss.at[t], tsr.at[t], zdev[1])

    def w_rows(yy):
        return pl.ds(pl.multiple_of(160 * yy, 32), 160)

    own_w = w_hbm.at[pl.ds(pl.multiple_of(640 * seat + 160 * y, 32), 160), :]
    ring, wy = {}, {}

    def w_ring(step, i, index):
        zz = z_of((-sign if i == 0 else sign) * step)
        slot = wa.at[w_rows(y), lanes(zz)]
        ring[index] = go(own_w if step == 0 else slot, slot, wzs.at[index], wzr.at[index], zdev[i])

    def w_share(m):
        slot = wa.at[w_rows(y), lanes(z_from[m])]
        for i in range(2):
            wy[m, i] = go(own_w if m == 0 else slot, slot, wys.at[m, i], wyr.at[m, i], ydev[i])

    def w_relay(m):
        got(wy[m, 0])
        slot = wa.at[w_rows(y_of(-sign)), lanes(z_from[m])]
        wy[m, 2] = go(slot, slot, wys.at[m, 2], wyr.at[m, 2], ydev[0])

    def w_forward(m):
        got(ring[m])
        k = (m + 1) // 2
        if m % 2 == 1 and k < 4:
            w_ring(k, 0, m + 2)
        if m % 2 == 0 and k < 3:
            w_ring(k, 1, m + 2)

    gx, gsib = {}, {}

    def g_block(xx):
        return ga.at[g_rows(2 * xx + core), :]

    def g_share():
        for c in st["ga"]:
            got(c)
        blk = g_block(x)
        for i in range(2):
            gx[i] = go(blk, blk, gxs.at[i], gxr.at[i], xdev[i])
        gsib[0] = go(blk, blk, gss.at[0], gsr.at[0], sibling)

    def g_pass(i):
        got(gx[i])
        blk = g_block(x_of((-sign, sign, 2)[i]))
        if i == 0:
            gx[2] = go(blk, blk, gxs.at[2], gxr.at[2], xdev[0])
        gsib[i + 1] = go(blk, blk, gss.at[i + 1], gsr.at[i + 1], sibling)

    def merge(cb, ms, factors=False):
        grads = [g_ref[g_rows(z_from[m]), :] for m in ms]
        rows = [xa[z_from[m], :, x_lanes(cb)] for m in ms]
        if factors:
            grads.append(qst[...])
            rows.append(pst[cb])
        before = f_ref[f_rows(cb), :].astype(F32) if 0 in ms else acc[cb]
        return before + mm(jnp.concatenate(rows, axis=0), jnp.concatenate(grads, axis=0), TN)

    def columns(ms):
        if 0 in ms:
            for i in range(4):
                got(gsib[i])
        for m in ms:
            got(wy[m, 1])
            got(wy[m, 2])

        @pl.loop(0, 2)
        def _(i):
            rows = pl.ds(pl.multiple_of(256 * i, 256), 256)
            v = sum(mm(ga[rows, lanes(z_from[m])], wa[:, lanes(z_from[m])], NT) for m in ms)
            if 0 in ms:
                cols[rows, :] = v
            else:
                ob[rows, :] = (cols[rows, :] + v).astype(BF16)

    st = {}

    def start():
        loads = [
            pltpu.make_async_copy(q_hbm, q_ref, lsem.at[0]),
            pltpu.make_async_copy(g_hbm, g_ref, lsem.at[1]),
            pltpu.make_async_copy(x_hbm, xa.at[z], lsem.at[2]),
            pltpu.make_async_copy(f_hbm, f_ref, lsem.at[3]),
            pltpu.make_async_copy(own_w, wa.at[w_rows(y), lanes(z)], lsem.at[4]),
        ]
        for c in loads:
            c.start()
        barrier = pltpu.get_barrier_semaphore()
        peers = [(dp, z_of(k)) for k in range(1, NZ)]
        peers += [(2 * p_of(k) + core, z) for k in range(1, NP)]
        peers += [at(y, x_of(k), 1 - core, z) for k in range(NX)]
        for peer in peers:
            pl.semaphore_signal(barrier, 1, device_id=peer, device_id_type=MESH)
        loads[0].wait()
        st["qs"] = qs = stack3(q_ref[...])
        loads[1].wait()
        h = fold3(mm(qs, g_ref[...], NT))
        for s in range(NZ):
            v = h[:, 64 * s : 64 * s + 64]
            hb[s] = jnp.concatenate([v[:16], v[16:]], axis=1)
        pl.semaphore_wait(barrier, len(peers))
        st["h"] = []
        for k in range(1, NZ):
            zd = z_of(k)
            st["h"].append(go(hb.at[zd], hr.at[k], hs.at[k], hrs.at[k], (dp, zd)))
        w_ring(0, 0, 1)
        w_ring(0, 1, 2)
        st["ga"] = []
        for k in range(1, NZ):
            zd = z_of(k)
            slot = ga.at[g_rows(seat), lanes(z)]
            st["ga"].append(go(g_ref.at[g_rows(zd), :], slot, gas.at[k], gar.at[k], (dp, zd)))
        w_share(0)
        ga[g_rows(seat), lanes(z)] = g_ref[g_rows(z), :]
        for c in loads[2:]:
            c.wait()
        tick(0)

    def left():
        qs = st["qs"]

        @pl.loop(0, 8)
        def _(cb):
            v = fold3(mm(qs, f_ref[f_rows(cb), :], NT))
            for a in range(4):
                pb[a, cb] = v[8 * a : 8 * a + 8]

        for c in st["h"]:
            got(c)
        hsum = hb[z]
        for k in range(1, NZ):
            hsum = hsum + hr[k]
        hparts = stack3(jnp.concatenate([hsum[:, :64], hsum[:, 64:]], axis=0))

        @pl.loop(0, 8)
        def _(cb):
            v = fold3(mm(hparts, xa[z, :, x_lanes(cb)], NN))
            for a in range(4):
                pb[a, cb] = pb[a, cb] + v[8 * a : 8 * a + 8]

    def sum_cores():
        c = go(pb.at[pl.ds(2 * (1 - core), 2)], pcr, cs.at[0], crs.at[0], sibling)
        w_forward(1)
        w_forward(2)
        got(c)

        @pl.loop(0, 8)
        def _(cb):
            for hh in range(2):
                ph[8 * hh + cb] = pb[2 * core + hh, cb] + pcr[hh, cb]

    def sum_plane():
        copies = []
        for k in range(1, NP):
            pd = p_of(k)
            copies.append(go(ph.at[pd], ppr.at[k], rss.at[k], rsr.at[k], (2 * pd + core, z)))
        g_share()
        w_share(1)
        w_share(2)
        for c in copies:
            got(c)
        total = ph[plane]
        for k in range(1, NP):
            total = total + ppr[k]
        for r in range(NZ):
            zb[r] = total[r : r + 1]

    def sum_ring():
        copies = []
        for k in range(1, NZ):
            zd = z_of(k)
            copies.append(go(zb.at[zd], pzr.at[k], zs.at[k], zr.at[k], (dp, zd)))
        tick(1)
        for c in copies:
            got(c)
        total = zb[z]
        for k in range(1, NZ):
            total = total + pzr[k]
        zf[z] = total
        own = zf.at[z]
        copies = [go(own, own, zgs.at[k], zgr.at[k], (dp, z_of(k))) for k in range(1, NZ)]
        w_forward(3)
        w_forward(4)
        tick(2)
        w_share(3)
        w_share(4)
        w_relay(0)
        for c in copies:
            got(c)
        pfin[core, plane] = jnp.concatenate([zf[r] for r in range(NZ)], axis=0)

    def spread():
        own = pfin.at[core, plane]
        copies = []
        for k in range(1, NP):
            copies.append(go(own, own, ags.at[k], agr.at[k], (2 * p_of(k) + core, z)))
        tick(3)
        w_relay(1)
        g_pass(0)
        g_pass(1)
        w_forward(5)
        w_forward(6)
        for c in copies:
            got(c)
        half = pfin.at[core]
        c = go(half, half, cs.at[1], crs.at[1], sibling)
        w_share(5)
        w_share(6)
        tick(4)
        got(c)

    def right():
        def block(cb, carry):
            gram, yt = carry
            parts = stack3(
                jnp.concatenate([pfin[a // 2, 8 * (a % 2) + cb] for a in range(4)], axis=0)
            )
            ps[cb] = parts
            gram = gram + mm(parts, parts, NT)
            yt = yt + mm(parts, xa[z, :, x_lanes(cb)], NT)
            return gram, yt

        gram, yt = lax.fori_loop(
            0, 8, block, (jnp.zeros((96, 96), F32), jnp.zeros((96, 64), F32))
        )
        yt = fold3(yt)
        gram = fold3(gram)
        st["gram"] = gram[:, 0:R] + gram[:, R : 2 * R] + gram[:, 2 * R : 3 * R]
        yb[...] = jnp.concatenate([yt[:16], yt[16:]], axis=1)
        copies = [go(yb, yr.at[k], ys.at[k], yrs.at[k], (dp, z_of(k))) for k in range(1, NZ)]
        w_forward(7)
        w_share(7)
        tick(5)
        w_relay(2)
        w_relay(3)
        qt = lax.fori_loop(
            0, 8, lambda cb, t: t + mm(ps[cb], f_ref[f_rows(cb), :], NN), jnp.zeros((96, 384), F32)
        )
        qt = qt + mm(stack3(yt), g_ref[g_rows(z), :], NN)
        linv = inverse_factor(st["gram"])
        st["l"] = jnp.concatenate(
            [jnp.concatenate([part] * 3, axis=1) for part in split3(linv)], axis=0
        )
        g_pass(2)
        for c in copies:
            got(c)
        for k in range(1, NZ):
            v = yr[k]
            yk = stack3(jnp.concatenate([v[:, :64], v[:, 64:]], axis=0))
            qt = qt + mm(yk, g_ref[g_rows(z_of(-k)), :], NN)
        qt = fold3(qt)
        for cc in range(2):
            qb[cc] = qt[16 * cc : 16 * cc + 16]

    def sum_right():
        c = go(qb.at[1 - core], qcr, cs.at[2], crs.at[2], sibling)
        tick(6)
        got(c)
        own = qp.at[plane]
        own[...] = qb[core] + qcr[...]
        copies = []
        for k in range(1, NP):
            copies.append(go(own, own, qps.at[k], qpr_s.at[k], (2 * p_of(k) + core, z)))
        tick(7)
        w_relay(4)
        w_relay(5)
        lparts = st["l"]

        @pl.loop(0, 8)
        def _(cb):
            hi, mid, low = split3(fold3(mm(lparts, ps[cb], NN)))
            pst[cb] = jnp.concatenate([hi, hi, hi, mid, mid, low], axis=0)

        tick(8)

        @pl.loop(0, 8)
        def _(cb):
            acc[cb] = merge(cb, [0, 1, 2])

        for c in copies:
            got(c)
        total = qp[0]
        for p in range(1, NP):
            total = total + qp[p]
        own = qfin.at[core]
        own[...] = total
        c = go(own, own, cs.at[3], crs.at[3], sibling)
        w_relay(6)
        w_relay(7)
        tick(9)
        columns([0, 1, 2, 3])
        got(c)
        qall = stack3(jnp.concatenate([qfin[0], qfin[1]], axis=0))
        qn = fold3(mm(lparts, qall, NN)) * (1.0 / 32.0)
        qn_ref[...] = qn
        hi, mid, low = split3(-qn)
        qst[...] = jnp.concatenate([hi, mid, low, hi, mid, hi], axis=0)

    def finish():
        tick(10)
        columns([4, 5, 6, 7])
        own_cols = pl.ds(pl.multiple_of(640 * seat, 128), 640)
        out = []
        for dx in range(NX):
            for other in range(2):
                if dx == 0 and other == 0:
                    continue
                i = 2 * dx + other
                xd = x_of(dx)
                cd = core if other == 0 else 1 - core
                out.append(
                    go(
                        ob.at[g_rows(2 * xd + cd), :], ig_ref.at[:, own_cols],
                        oxs.at[i], oxr.at[i], at(y, xd, cd, z),
                    )
                )
        ig_ref[:, own_cols] = ob[g_rows(seat), :]
        tick(11)

        @pl.loop(0, 8)
        def _(cb):
            acc[cb] = merge(cb, [3, 4], factors=True)

        for t in range(12, 16):
            tick(t)
        for t in range(4):
            got(tl[12 + t])

            @pl.loop(2 * t, 2 * t + 2)
            def _(cb):
                nf_ref[f_rows(cb), :] = merge(cb, [5, 6, 7]).astype(BF16)

        for c in out:
            got(c)

    steps = [
        start, left, sum_cores, sum_plane, sum_ring, spread, right, sum_right, finish,
    ]
    for step in steps:
        step()
    for c in sent:
        c.wait_send()


def store_kernel(a, b, c, a_out, b_out, c_out, sems):
    copies = [
        pltpu.make_async_copy(src, dst, sems.at[i])
        for i, (src, dst) in enumerate(((a, a_out), (b, b_out), (c, c_out)))
    ]
    for copy in copies:
        copy.start()
    for copy in copies:
        copy.wait()


def local(tokens, token_grads, weight, feedback, q_start):
    vmem = pl.BlockSpec(memory_space=pltpu.VMEM)
    hbm = pl.BlockSpec(memory_space=pl.ANY)
    dma = pltpu.SemaphoreType.DMA
    operands = (tokens, token_grads, q_start.T, weight, feedback[0])
    input_grads, new_feedback, q_next = pl.pallas_call(
        main_kernel,
        name="all_steps",
        out_shape=(
            jax.ShapeDtypeStruct((64, 5120), BF16),
            jax.ShapeDtypeStruct((5120, 384), BF16),
            jax.ShapeDtypeStruct((R, 384), F32),
        ),
        in_specs=[pl.BlockSpec(memory_space=pltpu.HBM)] * 5,
        out_specs=(vmem, vmem, vmem),
        scratch_shapes=[
            pltpu.VMEM((512, 384), BF16),
            pltpu.VMEM((R, 384), F32),
            pltpu.VMEM((5120, 384), BF16),
            pltpu.VMEM((NZ, 64, 5120), BF16),
            pltpu.VMEM((8, 640, 384), F32),
            pltpu.VMEM((8, 192, 640), BF16),
            pltpu.VMEM((192, 384), BF16),
            pltpu.VMEM((NZ, 16, 128), F32),
            pltpu.VMEM((NZ, 16, 128), F32),
            pltpu.VMEM((4, 8, 8, 640), F32),
            pltpu.VMEM((2, 8, 8, 640), F32),
            pltpu.VMEM((NP, 8, 640), F32),
            pltpu.VMEM((NP, 8, 640), F32),
            pltpu.VMEM((NZ, 1, 640), F32),
            pltpu.VMEM((NZ, 1, 640), F32),
            pltpu.VMEM((NZ, 1, 640), F32),
            pltpu.VMEM((2, NP, 8, 640), F32),
            pltpu.VMEM((8, 96, 640), BF16),
            pltpu.VMEM((16, 128), F32),
            pltpu.VMEM((NZ, 16, 128), F32),
            pltpu.VMEM((2, 16, 384), F32),
            pltpu.VMEM((16, 384), F32),
            pltpu.VMEM((NP, 16, 384), F32),
            pltpu.VMEM((2, 16, 384), F32),
            pltpu.VMEM((512, 3072), BF16),
            pltpu.VMEM((640, 3072), BF16),
            pltpu.VMEM((512, 640), F32),
            pltpu.VMEM((512, 640), BF16),
            dma((5,)),
            dma((NZ,)), dma((NZ,)),
            dma((4,)), dma((4,)),
            dma((NP,)), dma((NP,)),
            dma((NZ,)), dma((NZ,)),
            dma((NZ,)), dma((NZ,)),
            dma((NP,)), dma((NP,)),
            dma((NZ,)), dma((NZ,)),
            dma((NP,)), dma((NP,)),
            dma((NZ,)), dma((NZ,)),
            dma((3,)), dma((3,)),
            dma((4,)), dma((4,)),
            dma((8,)), dma((8,)),
            dma((8, 3)), dma((8, 3)),
            dma((8,)), dma((8,)),
            dma((16,)), dma((16,)),
            dma((12,)), dma((12,)),
        ],
        compiler_params=pltpu.CompilerParams(
            collective_id=0, has_side_effects=True, vmem_limit_bytes=42 * 2**20
        ),
        cost_estimate=pl.CostEstimate(flops=5 * 10**9, bytes_accessed=13 * 10**6, transcendentals=0),
    )(*(pltpu.with_memory_space_constraint(a, pltpu.HBM) for a in operands))
    results = (input_grads, new_feedback, q_next)
    input_grads, new_feedback, q_next = pl.pallas_call(
        store_kernel,
        name="store",
        out_shape=tuple(jax.ShapeDtypeStruct(r.shape, r.dtype) for r in results),
        in_specs=[vmem] * 3,
        out_specs=(hbm,) * 3,
        scratch_shapes=[dma((3,))],
        compiler_params=pltpu.CompilerParams(vmem_limit_bytes=2**20),
    )(*results)
    return input_grads, new_feedback[None], q_next.T


def solution(mesh):
    return jax.shard_map(
        local,
        mesh=mesh,
        in_specs=(
            P(("dp", "tensor"), None),
            P("dp", "tensor"),
            P(None, "tensor"),
            P("dp", None, "tensor"),
            P("tensor", None),
        ),
        out_specs=(P(("dp", "tensor"), None), P("dp", None, "tensor"), P("tensor", None)),
        check_vma=False,
    )
```

```python
import jax
import jax.numpy as jnp
from jax import lax
from jax.experimental import pallas as pl
from jax.experimental.pallas import tpu as pltpu
from jax.sharding import PartitionSpec as P

MESH = pl.DeviceIdType.MESH
F32 = jnp.float32
BF16 = jnp.bfloat16
NY, NX, NZ = 4, 4, 8
NP = NY * NX
R = 32
NN = (((1,), (0,)), ((), ()))
NT = (((1,), (1,)), ((), ()))
TN = (((0,), (0,)), ((), ()))


def mm(a, b, dims):
    return lax.dot_general(a, b, dims, preferred_element_type=F32)


def split3(v):
    hi = v.astype(BF16)
    rest = v - hi.astype(F32)
    mid = rest.astype(BF16)
    low = (rest - mid.astype(F32)).astype(BF16)
    return hi, mid, low


def stack3(v):
    return jnp.concatenate(split3(v), axis=0)


def fold3(v):
    return v[0:R] + v[R : 2 * R] + v[2 * R : 3 * R]


def inverse_factor(gram):
    rows = lax.broadcasted_iota(jnp.int32, (R, 1), 0)
    eye = (
        lax.broadcasted_iota(jnp.int32, (R, R), 0)
        == lax.broadcasted_iota(jnp.int32, (R, R), 1)
    ).astype(F32)
    a = jnp.concatenate([gram, eye], axis=1)
    for j in range(R):
        row = a[j : j + 1, :]
        pivot = a[j : j + 1, j : j + 1]
        factor = jnp.where(rows > j, a[:, j : j + 1] / pivot, 0.0)
        a = a - factor * row
    diag = jnp.sum(a[:, :R] * eye, axis=1, keepdims=True)
    return a[:, R:] / jnp.sqrt(diag)


def main_kernel(
    x_hbm, g_hbm, q_hbm, w_hbm, f_hbm,
    ig_ref, nf_ref, qn_ref,
    g_ref, q_ref, f_ref, xa, acc, pst, qst, hb, hr, pb, pcr, ph, ppr, zb, pzr, zf, pfin, ps, yb, yr,
    qb, qcr, qp, qfin, ga, wa, cols, ob,
    lsem, hs, hrs, cs, crs, rss, rsr, zs, zr, zgs, zgr, ags, agr, ys, yrs, qps, qpr_s,
    gas, gar, gxs, gxr, gss, gsr, wzs, wzr, wys, wyr, oxs, oxr, tls, tlr, tss, tsr,
):
    dp = lax.axis_index("dp")
    z = lax.axis_index("tensor")
    plane = dp // 2
    core = lax.rem(dp, 2)
    y, x = plane // NX, lax.rem(plane, NX)
    sign = 1 - 2 * core
    seat = 2 * x + core

    def at(yy, xx, cc, zz):
        return ((yy * NX + xx) * 2 + cc, zz)

    def z_of(k):
        return lax.rem(z + k + 2 * NZ, NZ)

    def x_of(k):
        return lax.rem(x + k + 2 * NX, NX)

    def y_of(k):
        return lax.rem(y + k + 2 * NY, NY)

    def p_of(k):
        return lax.rem(plane + k, NP)

    sent, pending, settled = [], {}, [0, 0]

    def go(src, dst, s_sem, r_sem, device):
        copy = pltpu.make_async_remote_copy(
            src_ref=src, dst_ref=dst, send_sem=s_sem, recv_sem=r_sem,
            device_id=device, device_id_type=MESH,
        )
        copy.start()
        sent.append(copy)
        pending[id(copy)] = copy
        return copy

    def settle():
        while settled[0] < settled[1]:
            sent[settled[0]].wait_send()
            settled[0] += 1
        settled[1] = len(sent)

    def got(copy):
        copy.wait_recv()
        del pending[id(copy)]

    sibling = (2 * plane + 1 - core, z)

    def g_rows(s):
        return pl.ds(pl.multiple_of(64 * s, 64), 64)

    def lanes(zz):
        return pl.ds(pl.multiple_of(384 * zz, 128), 384)

    def f_rows(cb):
        return pl.ds(pl.multiple_of(640 * cb, 640), 640)

    def x_lanes(cb):
        return pl.ds(pl.multiple_of(640 * cb, 128), 640)

    z_from = [z] + [z_of(d * k * sign) for k in range(1, 4) for d in (-1, 1)] + [z_of(4)]
    xdev = [at(y, x_of(sign), core, z), at(y, x_of(-sign), core, z)]
    ydev = [at(y_of(sign), x, core, z), at(y_of(-sign), x, core, z)]
    zdev = [(dp, z_of(sign)), (dp, z_of(-sign))]

    tl, ts = {}, {}

    def tick(t):
        k, part = t // 4, pl.ds(1280 * (t % 4), 1280)
        if k > 0:
            got(tl[t - 4])
        out = xa.at[z_of(-sign * k), :, part]
        tl[t] = go(out, out, tls.at[t], tlr.at[t], zdev[0])
        if k > 0 and t - 4 in ts:
            got(ts[t - 4])
        if k < 3:
            out = xa.at[z_of(sign * k), :, part]
            ts[t] = go(out, out, tss.at[t], tsr.at[t], zdev[1])

    def w_rows(yy):
        return pl.ds(pl.multiple_of(160 * yy, 32), 160)

    own_w = w_hbm.at[pl.ds(pl.multiple_of(640 * seat + 160 * y, 32), 160), :]
    ring, wy = {}, {}

    def w_ring(step, i, index):
        zz = z_of((-sign if i == 0 else sign) * step)
        slot = wa.at[w_rows(y), lanes(zz)]
        ring[index] = go(own_w if step == 0 else slot, slot, wzs.at[index], wzr.at[index], zdev[i])

    def w_share(m):
        slot = wa.at[w_rows(y), lanes(z_from[m])]
        for i in range(2):
            wy[m, i] = go(own_w if m == 0 else slot, slot, wys.at[m, i], wyr.at[m, i], ydev[i])

    def w_relay(m):
        got(wy[m, 0])
        slot = wa.at[w_rows(y_of(-sign)), lanes(z_from[m])]
        wy[m, 2] = go(slot, slot, wys.at[m, 2], wyr.at[m, 2], ydev[0])

    def w_forward(m):
        got(ring[m])
        k = (m + 1) // 2
        if m % 2 == 1 and k < 4:
            w_ring(k, 0, m + 2)
        if m % 2 == 0 and k < 3:
            w_ring(k, 1, m + 2)

    gx, gsib = {}, {}

    def g_block(xx):
        return ga.at[g_rows(2 * xx + core), :]

    def g_share():
        for c in st["ga"]:
            got(c)
        blk = g_block(x)
        for i in range(2):
            gx[i] = go(blk, blk, gxs.at[i], gxr.at[i], xdev[i])
        gsib[0] = go(blk, blk, gss.at[0], gsr.at[0], sibling)

    def g_pass(i):
        got(gx[i])
        blk = g_block(x_of((-sign, sign, 2)[i]))
        if i == 0:
            gx[2] = go(blk, blk, gxs.at[2], gxr.at[2], xdev[0])
        gsib[i + 1] = go(blk, blk, gss.at[i + 1], gsr.at[i + 1], sibling)

    def merge(cb, ms, factors=False):
        grads = [g_ref[g_rows(z_from[m]), :] for m in ms]
        rows = [xa[z_from[m], :, x_lanes(cb)] for m in ms]
        if factors:
            grads.append(qst[...])
            rows.append(pst[cb])
        before = f_ref[f_rows(cb), :].astype(F32) if 0 in ms else acc[cb]
        return before + mm(jnp.concatenate(rows, axis=0), jnp.concatenate(grads, axis=0), TN)

    def columns(ms):
        if 0 in ms:
            for i in range(4):
                got(gsib[i])
        for m in ms:
            got(wy[m, 1])
            got(wy[m, 2])

        @pl.loop(0, 2)
        def _(i):
            rows = pl.ds(pl.multiple_of(256 * i, 256), 256)
            v = sum(mm(ga[rows, lanes(z_from[m])], wa[:, lanes(z_from[m])], NT) for m in ms)
            if 0 in ms:
                cols[rows, :] = v
            else:
                ob[rows, :] = (cols[rows, :] + v).astype(BF16)

    def send_columns():
        own_cols = pl.ds(pl.multiple_of(640 * seat, 128), 640)
        st["out"] = []
        for dx in range(NX):
            for other in range(2):
                if dx == 0 and other == 0:
                    continue
                i = 2 * dx + other
                xd = x_of(dx)
                cd = core if other == 0 else 1 - core
                st["out"].append(
                    go(
                        ob.at[g_rows(2 * xd + cd), :], ig_ref.at[:, own_cols],
                        oxs.at[i], oxr.at[i], at(y, xd, cd, z),
                    )
                )
        ig_ref[:, own_cols] = ob[g_rows(seat), :]

    st = {}

    def start():
        loads = [
            pltpu.make_async_copy(q_hbm, q_ref, lsem.at[0]),
            pltpu.make_async_copy(g_hbm, g_ref, lsem.at[1]),
            pltpu.make_async_copy(x_hbm, xa.at[z], lsem.at[2]),
            pltpu.make_async_copy(f_hbm, f_ref, lsem.at[3]),
            pltpu.make_async_copy(own_w, wa.at[w_rows(y), lanes(z)], lsem.at[4]),
        ]
        for c in loads:
            c.start()
        barrier = pltpu.get_barrier_semaphore()
        peers = [(dp, z_of(k)) for k in range(1, NZ)]
        peers += [(2 * p_of(k) + core, z) for k in range(1, NP)]
        peers += [at(y, x_of(k), 1 - core, z) for k in range(NX)]
        for peer in peers:
            pl.semaphore_signal(barrier, 1, device_id=peer, device_id_type=MESH)
        loads[0].wait()
        st["qs"] = qs = stack3(q_ref[...])
        loads[1].wait()
        h = fold3(mm(qs, g_ref[...], NT))
        for s in range(NZ):
            v = h[:, 64 * s : 64 * s + 64]
            hb[s] = jnp.concatenate([v[:16], v[16:]], axis=1)
        pl.semaphore_wait(barrier, len(peers))
        st["h"] = []
        for k in range(1, NZ):
            zd = z_of(k)
            st["h"].append(go(hb.at[zd], hr.at[k], hs.at[k], hrs.at[k], (dp, zd)))
        w_ring(0, 0, 1)
        w_ring(0, 1, 2)
        st["ga"] = []
        for k in range(1, NZ):
            zd = z_of(k)
            slot = ga.at[g_rows(seat), lanes(z)]
            st["ga"].append(go(g_ref.at[g_rows(zd), :], slot, gas.at[k], gar.at[k], (dp, zd)))
        w_share(0)
        ga[g_rows(seat), lanes(z)] = g_ref[g_rows(z), :]
        for c in loads[2:]:
            c.wait()

    def left():
        qs = st["qs"]

        @pl.loop(0, 8)
        def _(cb):
            v = fold3(mm(qs, f_ref[f_rows(cb), :], NT))
            for a in range(4):
                pb[a, cb] = v[8 * a : 8 * a + 8]

        for c in st["h"]:
            got(c)
        hsum = hb[z]
        for k in range(1, NZ):
            hsum = hsum + hr[k]
        hparts = stack3(jnp.concatenate([hsum[:, :64], hsum[:, 64:]], axis=0))

        @pl.loop(0, 8)
        def _(cb):
            v = fold3(mm(hparts, xa[z, :, x_lanes(cb)], NN))
            for a in range(4):
                pb[a, cb] = pb[a, cb] + v[8 * a : 8 * a + 8]

    def sum_cores():
        c = go(pb.at[pl.ds(2 * (1 - core), 2)], pcr, cs.at[0], crs.at[0], sibling)
        w_forward(1)
        w_forward(2)
        tick(0)
        got(c)

        @pl.loop(0, 8)
        def _(cb):
            for hh in range(2):
                ph[8 * hh + cb] = pb[2 * core + hh, cb] + pcr[hh, cb]

    def sum_plane():
        copies = []
        for k in range(1, NP):
            pd = p_of(k)
            copies.append(go(ph.at[pd], ppr.at[k], rss.at[k], rsr.at[k], (2 * pd + core, z)))
        g_share()
        w_share(1)
        w_share(2)
        w_forward(3)
        w_forward(4)
        for c in copies:
            got(c)
        total = ph[plane]
        for k in range(1, NP):
            total = total + ppr[k]
        for r in range(NZ):
            zb[r] = total[r : r + 1]

    def sum_ring():
        copies = []
        for k in range(1, NZ):
            zd = z_of(k)
            copies.append(go(zb.at[zd], pzr.at[k], zs.at[k], zr.at[k], (dp, zd)))
        tick(1)
        w_share(3)
        w_share(4)
        w_relay(0)
        for c in copies:
            got(c)
        total = zb[z]
        for k in range(1, NZ):
            total = total + pzr[k]
        zf[z] = total
        own = zf.at[z]
        copies = [go(own, own, zgs.at[k], zgr.at[k], (dp, z_of(k))) for k in range(1, NZ)]
        w_forward(5)
        w_forward(6)
        tick(2)
        tick(3)
        w_share(5)
        w_share(6)
        w_relay(1)
        settle()
        for c in copies:
            got(c)
        pfin[core, plane] = jnp.concatenate([zf[r] for r in range(NZ)], axis=0)

    def spread():
        own = pfin.at[core, plane]
        copies = []
        for k in range(1, NP):
            copies.append(go(own, own, ags.at[k], agr.at[k], (2 * p_of(k) + core, z)))
        w_forward(7)
        tick(4)
        tick(5)
        w_share(7)
        w_relay(2)
        g_pass(0)
        g_pass(1)
        w_relay(3)
        settle()
        for c in copies:
            got(c)
        half = pfin.at[core]
        c = go(half, half, cs.at[1], crs.at[1], sibling)
        tick(6)
        g_pass(2)
        w_relay(4)
        got(c)

    def right():
        def block(cb, carry):
            gram, yt = carry
            parts = stack3(
                jnp.concatenate([pfin[a // 2, 8 * (a % 2) + cb] for a in range(4)], axis=0)
            )
            ps[cb] = parts
            gram = gram + mm(parts, parts, NT)
            yt = yt + mm(parts, xa[z, :, x_lanes(cb)], NT)
            return gram, yt

        gram, yt = lax.fori_loop(
            0, 8, block, (jnp.zeros((96, 96), F32), jnp.zeros((96, 64), F32))
        )
        yt = fold3(yt)
        gram = fold3(gram)
        st["gram"] = gram[:, 0:R] + gram[:, R : 2 * R] + gram[:, 2 * R : 3 * R]
        yb[...] = jnp.concatenate([yt[:16], yt[16:]], axis=1)
        copies = [go(yb, yr.at[k], ys.at[k], yrs.at[k], (dp, z_of(k))) for k in range(1, NZ)]
        tick(7)
        for m in range(5, 8):
            w_relay(m)
        qt = lax.fori_loop(
            0, 8, lambda cb, t: t + mm(ps[cb], f_ref[f_rows(cb), :], NN), jnp.zeros((96, 384), F32)
        )
        qt = qt + mm(stack3(yt), g_ref[g_rows(z), :], NN)
        linv = inverse_factor(st["gram"])
        st["l"] = jnp.concatenate(
            [jnp.concatenate([part] * 3, axis=1) for part in split3(linv)], axis=0
        )
        tick(8)
        settle()
        columns([0, 1, 2, 3])
        for c in copies:
            got(c)
        for k in range(1, NZ):
            v = yr[k]
            yk = stack3(jnp.concatenate([v[:, :64], v[:, 64:]], axis=0))
            qt = qt + mm(yk, g_ref[g_rows(z_of(-k)), :], NN)
        qt = fold3(qt)
        for cc in range(2):
            qb[cc] = qt[16 * cc : 16 * cc + 16]

    def sum_right():
        c = go(qb.at[1 - core], qcr, cs.at[2], crs.at[2], sibling)
        tick(9)
        got(c)
        own = qp.at[plane]
        own[...] = qb[core] + qcr[...]
        copies = []
        for k in range(1, NP):
            copies.append(go(own, own, qps.at[k], qpr_s.at[k], (2 * p_of(k) + core, z)))
        tick(10)
        lparts = st["l"]

        @pl.loop(0, 8)
        def _(cb):
            hi, mid, low = split3(fold3(mm(lparts, ps[cb], NN)))
            pst[cb] = jnp.concatenate([hi, hi, hi, mid, mid, low], axis=0)

        columns([4, 5, 6, 7])
        send_columns()
        tick(11)

        @pl.loop(0, 8)
        def _(cb):
            acc[cb] = merge(cb, [0, 1, 2])

        settle()
        for c in copies:
            got(c)
        total = qp[0]
        for p in range(1, NP):
            total = total + qp[p]
        own = qfin.at[core]
        own[...] = total
        c = go(own, own, cs.at[3], crs.at[3], sibling)
        tick(12)

        @pl.loop(0, 8)
        def _(cb):
            acc[cb] = merge(cb, [3, 4])

        settle()
        got(c)
        qall = stack3(jnp.concatenate([qfin[0], qfin[1]], axis=0))
        qn = fold3(mm(lparts, qall, NN)) * (1.0 / 32.0)
        qn_ref[...] = qn
        hi, mid, low = split3(-qn)
        qst[...] = jnp.concatenate([hi, mid, low, hi, mid, hi], axis=0)

    def finish():
        for t in range(13, 16):
            tick(t)
        settle()
        for t in range(4):
            got(tl[12 + t])

            @pl.loop(2 * t, 2 * t + 2)
            def _(cb):
                nf_ref[f_rows(cb), :] = merge(cb, [5, 6, 7], factors=True).astype(BF16)

        for c in st["out"]:
            got(c)

    steps = [
        start, left, sum_cores, sum_plane, sum_ring, spread, right, sum_right, finish,
    ]
    for step in steps:
        step()
    settle()
    settle()


def store_kernel(a, b, c, a_out, b_out, c_out, sems):
    copies = [
        pltpu.make_async_copy(src, dst, sems.at[i])
        for i, (src, dst) in enumerate(((a, a_out), (b, b_out), (c, c_out)))
    ]
    for copy in copies:
        copy.start()
    for copy in copies:
        copy.wait()


def local(tokens, token_grads, weight, feedback, q_start):
    vmem = pl.BlockSpec(memory_space=pltpu.VMEM)
    hbm = pl.BlockSpec(memory_space=pl.ANY)
    dma = pltpu.SemaphoreType.DMA
    operands = (tokens, token_grads, q_start.T, weight, feedback[0])
    input_grads, new_feedback, q_next = pl.pallas_call(
        main_kernel,
        name="all_steps",
        out_shape=(
            jax.ShapeDtypeStruct((64, 5120), BF16),
            jax.ShapeDtypeStruct((5120, 384), BF16),
            jax.ShapeDtypeStruct((R, 384), F32),
        ),
        in_specs=[pl.BlockSpec(memory_space=pltpu.HBM)] * 5,
        out_specs=(vmem, vmem, vmem),
        scratch_shapes=[
            pltpu.VMEM((512, 384), BF16),
            pltpu.VMEM((R, 384), F32),
            pltpu.VMEM((5120, 384), BF16),
            pltpu.VMEM((NZ, 64, 5120), BF16),
            pltpu.VMEM((8, 640, 384), F32),
            pltpu.VMEM((8, 192, 640), BF16),
            pltpu.VMEM((192, 384), BF16),
            pltpu.VMEM((NZ, 16, 128), F32),
            pltpu.VMEM((NZ, 16, 128), F32),
            pltpu.VMEM((4, 8, 8, 640), F32),
            pltpu.VMEM((2, 8, 8, 640), F32),
            pltpu.VMEM((NP, 8, 640), F32),
            pltpu.VMEM((NP, 8, 640), F32),
            pltpu.VMEM((NZ, 1, 640), F32),
            pltpu.VMEM((NZ, 1, 640), F32),
            pltpu.VMEM((NZ, 1, 640), F32),
            pltpu.VMEM((2, NP, 8, 640), F32),
            pltpu.VMEM((8, 96, 640), BF16),
            pltpu.VMEM((16, 128), F32),
            pltpu.VMEM((NZ, 16, 128), F32),
            pltpu.VMEM((2, 16, 384), F32),
            pltpu.VMEM((16, 384), F32),
            pltpu.VMEM((NP, 16, 384), F32),
            pltpu.VMEM((2, 16, 384), F32),
            pltpu.VMEM((512, 3072), BF16),
            pltpu.VMEM((640, 3072), BF16),
            pltpu.VMEM((512, 640), F32),
            pltpu.VMEM((512, 640), BF16),
            dma((5,)),
            dma((NZ,)), dma((NZ,)),
            dma((4,)), dma((4,)),
            dma((NP,)), dma((NP,)),
            dma((NZ,)), dma((NZ,)),
            dma((NZ,)), dma((NZ,)),
            dma((NP,)), dma((NP,)),
            dma((NZ,)), dma((NZ,)),
            dma((NP,)), dma((NP,)),
            dma((NZ,)), dma((NZ,)),
            dma((3,)), dma((3,)),
            dma((4,)), dma((4,)),
            dma((8,)), dma((8,)),
            dma((8, 3)), dma((8, 3)),
            dma((8,)), dma((8,)),
            dma((16,)), dma((16,)),
            dma((12,)), dma((12,)),
        ],
        compiler_params=pltpu.CompilerParams(
            collective_id=0, has_side_effects=True, vmem_limit_bytes=42 * 2**20
        ),
        cost_estimate=pl.CostEstimate(flops=5 * 10**9, bytes_accessed=13 * 10**6, transcendentals=0),
    )(*(pltpu.with_memory_space_constraint(a, pltpu.HBM) for a in operands))
    results = (input_grads, new_feedback, q_next)
    input_grads, new_feedback, q_next = pl.pallas_call(
        store_kernel,
        name="store",
        out_shape=tuple(jax.ShapeDtypeStruct(r.shape, r.dtype) for r in results),
        in_specs=[vmem] * 3,
        out_specs=(hbm,) * 3,
        scratch_shapes=[dma((3,))],
        compiler_params=pltpu.CompilerParams(vmem_limit_bytes=2**20),
    )(*results)
    return input_grads, new_feedback[None], q_next.T


def solution(mesh):
    return jax.shard_map(
        local,
        mesh=mesh,
        in_specs=(
            P(("dp", "tensor"), None),
            P("dp", "tensor"),
            P(None, "tensor"),
            P("dp", None, "tensor"),
            P("tensor", None),
        ),
        out_specs=(P(("dp", "tensor"), None), P("dp", None, "tensor"), P("tensor", None)),
        check_vma=False,
    )
```

```python
import jax
import jax.numpy as jnp
from jax import lax
from jax.experimental import pallas as pl
from jax.experimental.pallas import tpu as pltpu
from jax.sharding import PartitionSpec as P

MESH = pl.DeviceIdType.MESH
F32 = jnp.float32
BF16 = jnp.bfloat16
NY, NX, NZ = 4, 4, 8
NP = NY * NX
R = 32
NN = (((1,), (0,)), ((), ()))
NT = (((1,), (1,)), ((), ()))
TN = (((0,), (0,)), ((), ()))


def mm(a, b, dims):
    return lax.dot_general(a, b, dims, preferred_element_type=F32)


def split3(v):
    hi = v.astype(BF16)
    rest = v - hi.astype(F32)
    mid = rest.astype(BF16)
    low = (rest - mid.astype(F32)).astype(BF16)
    return hi, mid, low


def stack3(v):
    return jnp.concatenate(split3(v), axis=0)


def fold3(v):
    return v[0:R] + v[R : 2 * R] + v[2 * R : 3 * R]


def inverse_factor(gram):
    rows = lax.broadcasted_iota(jnp.int32, (R, 1), 0)
    eye = (
        lax.broadcasted_iota(jnp.int32, (R, R), 0)
        == lax.broadcasted_iota(jnp.int32, (R, R), 1)
    ).astype(F32)
    a = jnp.concatenate([gram, eye], axis=1)
    for j in range(R):
        row = a[j : j + 1, :]
        pivot = a[j : j + 1, j : j + 1]
        factor = jnp.where(rows > j, a[:, j : j + 1] / pivot, 0.0)
        a = a - factor * row
    diag = jnp.sum(a[:, :R] * eye, axis=1, keepdims=True)
    return a[:, R:] / jnp.sqrt(diag)


def main_kernel(
    x_hbm, g_hbm, q_hbm, w_hbm, f_hbm,
    ig_ref, nf_ref, qn_ref,
    g_ref, q_ref, f_ref, xa, acc, pst, qst, hb, hr, pb, pcr, ph, ppr, zb, pzr, zf, pfin, ps, yb, yr,
    qb, qcr, qp, qfin, ga, wa, cols, ob,
    lsem, hs, hrs, cs, crs, rss, rsr, zs, zr, zgs, zgr, ags, agr, ys, yrs, qps, qpr_s,
    gas, gar, gxs, gxr, gss, gsr, wzs, wzr, wys, wyr, oxs, oxr, tls, tlr, tss, tsr,
):
    dp = lax.axis_index("dp")
    z = lax.axis_index("tensor")
    plane = dp // 2
    core = lax.rem(dp, 2)
    y, x = plane // NX, lax.rem(plane, NX)
    sign = 1 - 2 * core
    seat = 2 * x + core

    def at(yy, xx, cc, zz):
        return ((yy * NX + xx) * 2 + cc, zz)

    def z_of(k):
        return lax.rem(z + k + 2 * NZ, NZ)

    def x_of(k):
        return lax.rem(x + k + 2 * NX, NX)

    def y_of(k):
        return lax.rem(y + k + 2 * NY, NY)

    def p_of(k):
        return lax.rem(plane + k, NP)

    sent, pending, settled = [], {}, [0, 0]

    def go(src, dst, s_sem, r_sem, device):
        copy = pltpu.make_async_remote_copy(
            src_ref=src, dst_ref=dst, send_sem=s_sem, recv_sem=r_sem,
            device_id=device, device_id_type=MESH,
        )
        copy.start()
        sent.append(copy)
        pending[id(copy)] = copy
        return copy

    def settle():
        while settled[0] < settled[1]:
            sent[settled[0]].wait_send()
            settled[0] += 1
        settled[1] = len(sent)

    def got(copy):
        copy.wait_recv()
        del pending[id(copy)]

    sibling = (2 * plane + 1 - core, z)

    def g_rows(s):
        return pl.ds(pl.multiple_of(64 * s, 64), 64)

    def lanes(zz):
        return pl.ds(pl.multiple_of(384 * zz, 128), 384)

    def f_rows(cb):
        return pl.ds(pl.multiple_of(640 * cb, 640), 640)

    def x_lanes(cb):
        return pl.ds(pl.multiple_of(640 * cb, 128), 640)

    z_from = [z] + [z_of(d * k * sign) for k in range(1, 4) for d in (-1, 1)] + [z_of(4)]
    xdev = [at(y, x_of(sign), core, z), at(y, x_of(-sign), core, z)]
    ydev = [at(y_of(sign), x, core, z), at(y_of(-sign), x, core, z)]
    zdev = [(dp, z_of(sign)), (dp, z_of(-sign))]

    tl, ts = {}, {}

    def tick(t):
        k, part = t // 4, pl.ds(1280 * (t % 4), 1280)
        if k > 0:
            got(tl[t - 4])
        out = xa.at[z_of(-sign * k), :, part]
        tl[t] = go(out, out, tls.at[t], tlr.at[t], zdev[0])
        if k > 0 and t - 4 in ts:
            got(ts[t - 4])
        if k < 3:
            out = xa.at[z_of(sign * k), :, part]
            ts[t] = go(out, out, tss.at[t], tsr.at[t], zdev[1])

    def w_rows(yy):
        return pl.ds(pl.multiple_of(160 * yy, 32), 160)

    own_w = w_hbm.at[pl.ds(pl.multiple_of(640 * seat + 160 * y, 32), 160), :]
    ring, wy = {}, {}

    def w_ring(step, i, index):
        zz = z_of((-sign if i == 0 else sign) * step)
        slot = wa.at[w_rows(y), lanes(zz)]
        ring[index] = go(own_w if step == 0 else slot, slot, wzs.at[index], wzr.at[index], zdev[i])

    def w_share(m):
        slot = wa.at[w_rows(y), lanes(z_from[m])]
        for i in range(2):
            wy[m, i] = go(own_w if m == 0 else slot, slot, wys.at[m, i], wyr.at[m, i], ydev[i])

    def w_relay(m):
        got(wy[m, 0])
        slot = wa.at[w_rows(y_of(-sign)), lanes(z_from[m])]
        wy[m, 2] = go(slot, slot, wys.at[m, 2], wyr.at[m, 2], ydev[0])

    def w_forward(m):
        got(ring[m])
        k = (m + 1) // 2
        if m % 2 == 1 and k < 4:
            w_ring(k, 0, m + 2)
        if m % 2 == 0 and k < 3:
            w_ring(k, 1, m + 2)

    gx, gsib = {}, {}

    def g_block(xx):
        return ga.at[g_rows(2 * xx + core), :]

    def g_share():
        for c in st["ga"]:
            got(c)
        blk = g_block(x)
        for i in range(2):
            gx[i] = go(blk, blk, gxs.at[i], gxr.at[i], xdev[i])
        gsib[0] = go(blk, blk, gss.at[0], gsr.at[0], sibling)

    def g_pass(i):
        got(gx[i])
        blk = g_block(x_of((-sign, sign, 2)[i]))
        if i == 0:
            gx[2] = go(blk, blk, gxs.at[2], gxr.at[2], xdev[0])
        gsib[i + 1] = go(blk, blk, gss.at[i + 1], gsr.at[i + 1], sibling)

    def merge(cb, ms, factors=False):
        grads = [g_ref[g_rows(z_from[m]), :] for m in ms]
        rows = [xa[z_from[m], :, x_lanes(cb)] for m in ms]
        if factors:
            grads.append(qst[...])
            rows.append(pst[cb])
        before = f_ref[f_rows(cb), :].astype(F32) if 0 in ms else acc[cb]
        return before + mm(jnp.concatenate(rows, axis=0), jnp.concatenate(grads, axis=0), TN)

    def columns(ms):
        if 0 in ms:
            for i in range(4):
                got(gsib[i])
        for m in ms:
            got(wy[m, 1])
            got(wy[m, 2])

        @pl.loop(0, 2)
        def _(i):
            rows = pl.ds(pl.multiple_of(256 * i, 256), 256)
            v = sum(mm(ga[rows, lanes(z_from[m])], wa[:, lanes(z_from[m])], NT) for m in ms)
            if 0 in ms:
                cols[rows, :] = v
            else:
                ob[rows, :] = (cols[rows, :] + v).astype(BF16)

    def send_columns():
        own_cols = pl.ds(pl.multiple_of(640 * seat, 128), 640)
        st["out"] = []
        for dx in range(NX):
            for other in range(2):
                if dx == 0 and other == 0:
                    continue
                i = 2 * dx + other
                xd = x_of(dx)
                cd = core if other == 0 else 1 - core
                st["out"].append(
                    go(
                        ob.at[g_rows(2 * xd + cd), :], ig_ref.at[:, own_cols],
                        oxs.at[i], oxr.at[i], at(y, xd, cd, z),
                    )
                )
        ig_ref[:, own_cols] = ob[g_rows(seat), :]

    st = {}

    def start():
        loads = [
            pltpu.make_async_copy(q_hbm, q_ref, lsem.at[0]),
            pltpu.make_async_copy(g_hbm, g_ref, lsem.at[1]),
            pltpu.make_async_copy(x_hbm, xa.at[z], lsem.at[2]),
            pltpu.make_async_copy(f_hbm, f_ref, lsem.at[3]),
            pltpu.make_async_copy(own_w, wa.at[w_rows(y), lanes(z)], lsem.at[4]),
        ]
        for c in loads:
            c.start()
        barrier = pltpu.get_barrier_semaphore()
        peers = [(dp, z_of(k)) for k in range(1, NZ)]
        peers += [(2 * p_of(k) + core, z) for k in range(1, NP)]
        peers += [at(y, x_of(k), 1 - core, z) for k in range(NX)]
        for peer in peers:
            pl.semaphore_signal(barrier, 1, device_id=peer, device_id_type=MESH)
        loads[0].wait()
        st["qs"] = qs = stack3(q_ref[...])
        loads[1].wait()
        h = fold3(mm(qs, g_ref[...], NT))
        for s in range(NZ):
            v = h[:, 64 * s : 64 * s + 64]
            hb[s] = jnp.concatenate([v[:16], v[16:]], axis=1)
        pl.semaphore_wait(barrier, len(peers))
        st["h"] = []
        for k in range(1, NZ):
            zd = z_of(k)
            st["h"].append(go(hb.at[zd], hr.at[k], hs.at[k], hrs.at[k], (dp, zd)))
        w_ring(0, 0, 1)
        w_ring(0, 1, 2)
        st["ga"] = []
        for k in range(1, NZ):
            zd = z_of(k)
            slot = ga.at[g_rows(seat), lanes(z)]
            st["ga"].append(go(g_ref.at[g_rows(zd), :], slot, gas.at[k], gar.at[k], (dp, zd)))
        w_share(0)
        ga[g_rows(seat), lanes(z)] = g_ref[g_rows(z), :]
        for c in loads[2:]:
            c.wait()

    def left():
        qs = st["qs"]

        @pl.loop(0, 8)
        def _(cb):
            v = fold3(mm(qs, f_ref[f_rows(cb), :], NT))
            for a in range(4):
                pb[a, cb] = v[8 * a : 8 * a + 8]

        for c in st["h"]:
            got(c)
        hsum = hb[z]
        for k in range(1, NZ):
            hsum = hsum + hr[k]
        hparts = stack3(jnp.concatenate([hsum[:, :64], hsum[:, 64:]], axis=0))

        @pl.loop(0, 8)
        def _(cb):
            v = fold3(mm(hparts, xa[z, :, x_lanes(cb)], NN))
            for a in range(4):
                pb[a, cb] = pb[a, cb] + v[8 * a : 8 * a + 8]

    def sum_cores():
        c = go(pb.at[pl.ds(2 * (1 - core), 2)], pcr, cs.at[0], crs.at[0], sibling)
        w_forward(1)
        w_forward(2)
        tick(0)
        got(c)

        @pl.loop(0, 8)
        def _(cb):
            for hh in range(2):
                ph[8 * hh + cb] = pb[2 * core + hh, cb] + pcr[hh, cb]

    def sum_plane():
        copies = []
        for k in range(1, NP):
            pd = p_of(k)
            copies.append(go(ph.at[pd], ppr.at[k], rss.at[k], rsr.at[k], (2 * pd + core, z)))
        g_share()
        w_share(1)
        w_share(2)
        w_forward(3)
        w_forward(4)
        for c in copies:
            got(c)
        total = ph[plane]
        for k in range(1, NP):
            total = total + ppr[k]
        for r in range(NZ):
            zb[r] = total[r : r + 1]

    def sum_ring():
        copies = []
        for k in range(1, NZ):
            zd = z_of(k)
            copies.append(go(zb.at[zd], pzr.at[k], zs.at[k], zr.at[k], (dp, zd)))
        tick(1)
        w_share(3)
        w_share(4)
        w_relay(0)
        for c in copies:
            got(c)
        total = zb[z]
        for k in range(1, NZ):
            total = total + pzr[k]
        zf[z] = total
        own = zf.at[z]
        copies = [go(own, own, zgs.at[k], zgr.at[k], (dp, z_of(k))) for k in range(1, NZ)]
        w_forward(5)
        w_forward(6)
        tick(2)
        tick(3)
        w_share(5)
        w_share(6)
        w_relay(1)
        settle()
        for c in copies:
            got(c)
        pfin[core, plane] = jnp.concatenate([zf[r] for r in range(NZ)], axis=0)

    def spread():
        own = pfin.at[core, plane]
        copies = []
        for k in range(1, NP):
            copies.append(go(own, own, ags.at[k], agr.at[k], (2 * p_of(k) + core, z)))
        w_forward(7)
        tick(4)
        tick(5)
        w_share(7)
        w_relay(2)
        g_pass(0)
        g_pass(1)
        w_relay(3)
        settle()
        for c in copies:
            got(c)
        half = pfin.at[core]
        c = go(half, half, cs.at[1], crs.at[1], sibling)
        tick(6)
        g_pass(2)
        w_relay(4)
        got(c)

    def right():
        def block(cb, carry):
            gram, yt = carry
            parts = stack3(
                jnp.concatenate([pfin[a // 2, 8 * (a % 2) + cb] for a in range(4)], axis=0)
            )
            ps[cb] = parts
            gram = gram + mm(parts, parts, NT)
            yt = yt + mm(parts, xa[z, :, x_lanes(cb)], NT)
            return gram, yt

        gram, yt = lax.fori_loop(
            0, 8, block, (jnp.zeros((96, 96), F32), jnp.zeros((96, 64), F32))
        )
        yt = fold3(yt)
        gram = fold3(gram)
        st["gram"] = gram[:, 0:R] + gram[:, R : 2 * R] + gram[:, 2 * R : 3 * R]
        yb[...] = jnp.concatenate([yt[:16], yt[16:]], axis=1)
        copies = [go(yb, yr.at[k], ys.at[k], yrs.at[k], (dp, z_of(k))) for k in range(1, NZ)]
        tick(7)
        qt = lax.fori_loop(
            0, 8, lambda cb, t: t + mm(ps[cb], f_ref[f_rows(cb), :], NN), jnp.zeros((96, 384), F32)
        )
        qt = qt + mm(stack3(yt), g_ref[g_rows(z), :], NN)
        linv = inverse_factor(st["gram"])
        st["l"] = jnp.concatenate(
            [jnp.concatenate([part] * 3, axis=1) for part in split3(linv)], axis=0
        )
        for m in range(5, 8):
            w_relay(m)
        tick(8)
        settle()
        columns([0, 1, 2, 3])
        for c in copies:
            got(c)
        for k in range(1, NZ):
            v = yr[k]
            yk = stack3(jnp.concatenate([v[:, :64], v[:, 64:]], axis=0))
            qt = qt + mm(yk, g_ref[g_rows(z_of(-k)), :], NN)
        qt = fold3(qt)
        for cc in range(2):
            qb[cc] = qt[16 * cc : 16 * cc + 16]

    def sum_right():
        c = go(qb.at[1 - core], qcr, cs.at[2], crs.at[2], sibling)
        tick(9)
        got(c)
        own = qp.at[plane]
        own[...] = qb[core] + qcr[...]
        copies = []
        for k in range(1, NP):
            copies.append(go(own, own, qps.at[k], qpr_s.at[k], (2 * p_of(k) + core, z)))
        tick(10)
        lparts = st["l"]

        @pl.loop(0, 8)
        def _(cb):
            hi, mid, low = split3(fold3(mm(lparts, ps[cb], NN)))
            pst[cb] = jnp.concatenate([hi, hi, hi, mid, mid, low], axis=0)

        columns([4, 5, 6, 7])
        send_columns()
        tick(11)

        @pl.loop(0, 8)
        def _(cb):
            acc[cb] = merge(cb, [0, 1, 2])

        settle()
        for c in copies:
            got(c)
        total = qp[0]
        for p in range(1, NP):
            total = total + qp[p]
        own = qfin.at[core]
        own[...] = total
        c = go(own, own, cs.at[3], crs.at[3], sibling)
        tick(12)

        @pl.loop(0, 8)
        def _(cb):
            acc[cb] = merge(cb, [3, 4])

        settle()
        got(c)
        qall = stack3(jnp.concatenate([qfin[0], qfin[1]], axis=0))
        qn = fold3(mm(lparts, qall, NN)) * (1.0 / 32.0)
        qn_ref[...] = qn
        hi, mid, low = split3(-qn)
        qst[...] = jnp.concatenate([hi, mid, low, hi, mid, hi], axis=0)

    def finish():
        for t in range(13, 16):
            tick(t)
        settle()
        for t in range(4):
            got(tl[12 + t])

            @pl.loop(2 * t, 2 * t + 2)
            def _(cb):
                nf_ref[f_rows(cb), :] = merge(cb, [5, 6, 7], factors=True).astype(BF16)

        for c in st["out"]:
            got(c)

    steps = [
        start, left, sum_cores, sum_plane, sum_ring, spread, right, sum_right, finish,
    ]
    for step in steps:
        step()
    settle()
    settle()


def store_kernel(a, b, c, a_out, b_out, c_out, sems):
    copies = [
        pltpu.make_async_copy(src, dst, sems.at[i])
        for i, (src, dst) in enumerate(((a, a_out), (b, b_out), (c, c_out)))
    ]
    for copy in copies:
        copy.start()
    for copy in copies:
        copy.wait()


def local(tokens, token_grads, weight, feedback, q_start):
    vmem = pl.BlockSpec(memory_space=pltpu.VMEM)
    hbm = pl.BlockSpec(memory_space=pl.ANY)
    dma = pltpu.SemaphoreType.DMA
    operands = (tokens, token_grads, q_start.T, weight, feedback[0])
    input_grads, new_feedback, q_next = pl.pallas_call(
        main_kernel,
        name="all_steps",
        out_shape=(
            jax.ShapeDtypeStruct((64, 5120), BF16),
            jax.ShapeDtypeStruct((5120, 384), BF16),
            jax.ShapeDtypeStruct((R, 384), F32),
        ),
        in_specs=[pl.BlockSpec(memory_space=pltpu.HBM)] * 5,
        out_specs=(vmem, vmem, vmem),
        scratch_shapes=[
            pltpu.VMEM((512, 384), BF16),
            pltpu.VMEM((R, 384), F32),
            pltpu.VMEM((5120, 384), BF16),
            pltpu.VMEM((NZ, 64, 5120), BF16),
            pltpu.VMEM((8, 640, 384), F32),
            pltpu.VMEM((8, 192, 640), BF16),
            pltpu.VMEM((192, 384), BF16),
            pltpu.VMEM((NZ, 16, 128), F32),
            pltpu.VMEM((NZ, 16, 128), F32),
            pltpu.VMEM((4, 8, 8, 640), F32),
            pltpu.VMEM((2, 8, 8, 640), F32),
            pltpu.VMEM((NP, 8, 640), F32),
            pltpu.VMEM((NP, 8, 640), F32),
            pltpu.VMEM((NZ, 1, 640), F32),
            pltpu.VMEM((NZ, 1, 640), F32),
            pltpu.VMEM((NZ, 1, 640), F32),
            pltpu.VMEM((2, NP, 8, 640), F32),
            pltpu.VMEM((8, 96, 640), BF16),
            pltpu.VMEM((16, 128), F32),
            pltpu.VMEM((NZ, 16, 128), F32),
            pltpu.VMEM((2, 16, 384), F32),
            pltpu.VMEM((16, 384), F32),
            pltpu.VMEM((NP, 16, 384), F32),
            pltpu.VMEM((2, 16, 384), F32),
            pltpu.VMEM((512, 3072), BF16),
            pltpu.VMEM((640, 3072), BF16),
            pltpu.VMEM((512, 640), F32),
            pltpu.VMEM((512, 640), BF16),
            dma((5,)),
            dma((NZ,)), dma((NZ,)),
            dma((4,)), dma((4,)),
            dma((NP,)), dma((NP,)),
            dma((NZ,)), dma((NZ,)),
            dma((NZ,)), dma((NZ,)),
            dma((NP,)), dma((NP,)),
            dma((NZ,)), dma((NZ,)),
            dma((NP,)), dma((NP,)),
            dma((NZ,)), dma((NZ,)),
            dma((3,)), dma((3,)),
            dma((4,)), dma((4,)),
            dma((8,)), dma((8,)),
            dma((8, 3)), dma((8, 3)),
            dma((8,)), dma((8,)),
            dma((16,)), dma((16,)),
            dma((12,)), dma((12,)),
        ],
        compiler_params=pltpu.CompilerParams(
            collective_id=0, has_side_effects=True, vmem_limit_bytes=42 * 2**20
        ),
        cost_estimate=pl.CostEstimate(flops=5 * 10**9, bytes_accessed=13 * 10**6, transcendentals=0),
    )(*(pltpu.with_memory_space_constraint(a, pltpu.HBM) for a in operands))
    results = (input_grads, new_feedback, q_next)
    input_grads, new_feedback, q_next = pl.pallas_call(
        store_kernel,
        name="store",
        out_shape=tuple(jax.ShapeDtypeStruct(r.shape, r.dtype) for r in results),
        in_specs=[vmem] * 3,
        out_specs=(hbm,) * 3,
        scratch_shapes=[dma((3,))],
        compiler_params=pltpu.CompilerParams(vmem_limit_bytes=2**20),
    )(*results)
    return input_grads, new_feedback[None], q_next.T


def solution(mesh):
    return jax.shard_map(
        local,
        mesh=mesh,
        in_specs=(
            P(("dp", "tensor"), None),
            P("dp", "tensor"),
            P(None, "tensor"),
            P("dp", None, "tensor"),
            P("tensor", None),
        ),
        out_specs=(P(("dp", "tensor"), None), P("dp", None, "tensor"), P("tensor", None)),
        check_vma=False,
    )
```
